32 devices in a mesh: depth: 4 (over z), tile: 8 (over y, x, core).
Axes of the slice: x: 2, y: 2, z: 4, core: 2. Of those that a mesh axis runs over, the one named last changes fastest.
Arguments:
- transmission: float32 [2, 8, 2048, 512], P(None, 'depth', 'tile'), may hold values from -0.6 to 1.25, as said below
- probe: float32 [2, 256, 256], replicated, may hold values from -4.2 to 4.2
- intensity: float32 [16, 256, 256], P('tile'), may hold values from 0.25 to 4
- positions: int32 [16, 2], P('tile'), may hold values from 0 to 1792, as said below
- batch: int32 [16], P('tile'), may hold values from 0 to 1
Outputs:
- updated: float32 [2, 8, 2048, 512], P(None, 'depth', 'tile')
The draws below stay inside these ranges and needn't reach their ends.
Inputs may be any that keep to these rules, and one draw needn't show every extreme that they name: `positions`: probe j is held by tile device j // 2; its top row minus 256 times that device's index, plus half of 256, lies between 0 and 255; its left column is at most 256. On every tile device the window of its first probe starts at least 64 rows above the device's rows (unless clipped at the object's top) and the window of its second probe ends at least 64 rows below them (unless clipped at the object's bottom). `transmission`: the first component lies between 0.5 and 1.25, the second between -0.6 and 0.6.
All inputs are finite; a program needn't handle non-finite values.
Results may differ from the reference program's by a relative error of at most 0.0003.
Values sent between devices are 32-bit elements; how exact they have to be, the bound alone decides.
A program may use at most 192 MiB of HBM per device.

```python
import math
import jax
import jax.numpy as jnp
from jax import lax

PROBE = 256
ROWS_DEV = 256
COLS = 512
PROBES_DEV = 2
SLICES = 8
OBJ_ROWS = 2048
NPROB = 16


def draw_transmission(key, part):
    first, second = jax.random.split(jax.random.fold_in(key, 11))
    shape = (SLICES, OBJ_ROWS, COLS)
    real_part = jax.random.uniform(first, shape, jnp.float32, 0.6, 1.2)
    imag_part = jnp.clip(0.3 * jax.random.normal(second, shape, jnp.float32), -0.6, 0.6)
    return jnp.stack([real_part, imag_part], 0)


def draw_positions(key, part):
    first, second, third, fourth = jax.random.split(jax.random.fold_in(key, 23), 4)
    counter = jnp.arange(NPROB, dtype=jnp.int32)
    owner = counter // PROBES_DEV
    slot = counter % PROBES_DEV
    spread = jax.random.randint(first, (NPROB,), 0, ROWS_DEV, dtype=jnp.int32)
    upper = jax.random.randint(third, (NPROB,), 0, PROBE // 4 + 1, dtype=jnp.int32)
    lower = jax.random.randint(fourth, (NPROB,), ROWS_DEV - PROBE // 4, ROWS_DEV, dtype=jnp.int32)
    offset = jnp.where(slot == 0, upper, jnp.where(slot == 1, lower, spread))
    top_row = jnp.clip(owner * ROWS_DEV - PROBE // 2 + offset, 0, OBJ_ROWS - PROBE)
    left_col = jax.random.randint(second, (NPROB,), 0, COLS - PROBE + 1, dtype=jnp.int32)
    return jnp.stack([top_row, left_col], 1)


def place_ends(entries, stream_key, low, largest):
    longest = entries.shape.index(max(entries.shape))
    spots = []
    for shift in (0, 1):
        where = [jax.random.randint(jax.random.fold_in(stream_key, axis), (), 0, length) for axis, length in enumerate(entries.shape)]
        where[longest] = (where[longest] + shift) % entries.shape[longest]
        spots.append(tuple(where))
    return entries.at[spots[0]].set(low).at[spots[1]].set(largest)


def block_scale(rng, shape, pieces, low, high):
    def one(position, blocks):
        heights = jax.random.uniform(jax.random.fold_in(jax.random.fold_in(rng, 6), position), (blocks,), jnp.float32, low / len(pieces), high / len(pieces))
        return jnp.repeat(jnp.exp(heights), shape[position] // blocks).reshape((-1,) + (1,) * (len(shape) - position - 1))

    factor_of = one(*pieces[0])
    for cut in pieces[1:]:
        factor_of = factor_of * one(*cut)
    return factor_of


def normal_values(own_key, shape, width, reach, kind=jnp.bfloat16):
    entries = jax.random.normal(own_key, shape, jnp.float32) * width
    return jnp.minimum(jnp.maximum(entries, -reach), reach).astype(kind)


def setup_inputs(seed: int = 0) -> dict:
    key_list = jax.random.split(jax.random.key(seed), 6)
    transmission = draw_transmission(jax.random.fold_in(key_list[5], 71), 0)
    probe = normal_values(key_list[1], (2, PROBE, PROBE), 0.7, 4.2, jnp.float32)
    intensity = jnp.clip(jnp.exp(math.log(4.0) - 2.7725887 * jax.random.uniform(key_list[2], (NPROB, PROBE, PROBE), jnp.float32) ** block_scale(key_list[2], (NPROB, PROBE, PROBE), ((0, 8),), -0.2, 0.2)), 0.25, 4.0)
    positions = draw_positions(jax.random.fold_in(key_list[5], 71), 0)
    batch = place_ends(jax.random.randint(key_list[4], (NPROB,), 0, 2), jax.random.fold_in(key_list[4], 1), 0, 1).astype(jnp.int32)
    return {"transmission": transmission, "probe": probe, "intensity": intensity, "positions": positions, "batch": batch}


prop_strength = 24.0
step_rate = 0.08

def left_mul(matrix, field):
    return jnp.einsum('ij,...jk->...ik', matrix, field, precision=lax.Precision.HIGHEST)

def right_mul(field, matrix):
    return jnp.einsum('...ij,jk->...ik', field, matrix, precision=lax.Precision.HIGHEST)

def transform(field, operator_set):
    a_real, a_imag, b_real, b_imag = operator_set
    f_real, f_imag = field
    u_real = left_mul(a_real, f_real) - left_mul(a_imag, f_imag)
    u_imag = left_mul(a_real, f_imag) + left_mul(a_imag, f_real)
    return (right_mul(u_real, b_real) - right_mul(u_imag, b_imag), right_mul(u_real, b_imag) + right_mul(u_imag, b_real))

def product(first, second):
    return (first[0] * second[0] - first[1] * second[1], first[0] * second[1] + first[1] * second[0])

def operators(extent):
    counter = jnp.arange(extent, dtype=jnp.int32)
    phase = counter[:, None] * counter[None, :] % extent
    angles = phase.astype(jnp.float32) * (2.0 * math.pi / extent)
    norming = 1.0 / math.sqrt(extent)
    cosine = jnp.cos(angles) * norming
    sine = jnp.sin(angles) * norming
    freq = jnp.where(counter < extent // 2, counter, counter - extent).astype(jnp.float32) / extent
    turned = -math.pi * prop_strength * freq * freq
    h_real = jnp.cos(turned)
    h_imag = jnp.sin(turned)
    a_real = h_real[:, None] * cosine + h_imag[:, None] * sine
    a_imag = h_imag[:, None] * cosine - h_real[:, None] * sine
    highest = lax.Precision.HIGHEST
    q_real = jnp.dot(cosine, a_real, precision=highest) - jnp.dot(sine, a_imag, precision=highest)
    q_imag = jnp.dot(cosine, a_imag, precision=highest) + jnp.dot(sine, a_real, precision=highest)
    forward = (q_real, q_imag, q_real.T, q_imag.T)
    far_out = (cosine, -sine, cosine, -sine)
    return (forward, far_out)

def probe_loss(obj_patch, probe, measured, weight, forward, far_out):
    wavefront = (probe[0], probe[1])
    for layer in range(obj_patch.shape[1]):
        chi = product((obj_patch[0, layer], obj_patch[1, layer]), wavefront)
        wavefront = transform(chi, forward)
    far = transform(wavefront, far_out)
    resid = far[0] * far[0] + far[1] * far[1] - measured
    return weight * jnp.sum(resid * resid)

def reference(transmission, probe, intensity, positions, batch):
    forward, far_out = operators(PROBE)
    current = transmission
    for turn_at in range(2):

        def visit(grad_sum, number):
            zero = jnp.int32(0)
            start = (zero, zero, positions[number, 0], positions[number, 1])
            obj_patch = lax.dynamic_slice(current, start, (2, SLICES, PROBE, PROBE))
            weight = (batch[number] == turn_at).astype(jnp.float32)
            patch_grad = lax.cond(weight > 0, lambda: jax.grad(probe_loss)(obj_patch, probe, intensity[number], weight, forward, far_out), lambda: jnp.zeros_like(obj_patch))
            region = lax.dynamic_slice(grad_sum, start, (2, SLICES, PROBE, PROBE)) + patch_grad
            return (lax.dynamic_update_slice(grad_sum, region, start), None)
        grad_sum = lax.scan(visit, jnp.zeros_like(current), jnp.arange(NPROB, dtype=jnp.int32))[0]
        current = current - step_rate * grad_sum
    return current
```

```python
import functools
import math

import jax
import jax.numpy as jnp
import ml_dtypes
import numpy as np
from jax import lax
from jax.experimental import pallas as pl
from jax.experimental.pallas import tpu as pltpu
from jax.sharding import PartitionSpec as P

prop_strength = 24.0
step_rate = 0.08
MESH = pl.DeviceIdType.MESH
VMEM_LIMIT = 48 * 1024 * 1024


def operators(extent):
    counter = np.arange(extent)
    phase = (counter[:, None] * counter[None, :]) % extent
    angles = phase * (2.0 * math.pi / extent)
    fourier = (np.cos(angles) - 1j * np.sin(angles)) / math.sqrt(extent)
    freq = np.where(counter < extent // 2, counter, counter - extent) / extent
    chirp = np.exp(-1j * math.pi * prop_strength * freq * freq)
    forward = np.conj(fourier) @ (chirp[:, None] * fourier)
    forward = 0.5 * (forward + forward.T)
    packed = []
    for matrix in (forward, np.conj(forward), fourier, np.conj(fourier)):
        whole = np.block([[matrix.real, matrix.imag], [-matrix.imag, matrix.real]]).astype(np.float32)
        high = whole.astype(ml_dtypes.bfloat16)
        low = (whole - high.astype(np.float32)).astype(ml_dtypes.bfloat16)
        packed.append(np.stack([high, low]))
    return np.stack(packed)


def split(value):
    high = value.astype(jnp.bfloat16)
    return high, (value - high.astype(jnp.float32)).astype(jnp.bfloat16)


def dot(first, second):
    return jnp.dot(first, second, preferred_element_type=jnp.float32)


def transform(real, imag, op_ref, which):
    extent = real.shape[0]
    real_parts, imag_parts = split(real), split(imag)
    high, low = [
        jnp.concatenate([jnp.concatenate([r, i], 1), jnp.concatenate([-i, r], 1)], 0)
        for r, i in zip(real_parts, imag_parts)
    ]
    left_high, left_low = op_ref[which, 0, :extent], op_ref[which, 1, :extent]
    turned = dot(left_high, high) + (dot(left_high, low) + dot(left_low, high))
    high, low = split(turned)
    right_high, right_low = op_ref[which, 0], op_ref[which, 1]
    out = dot(high, right_high) + (dot(high, right_low) + dot(low, right_high))
    return out[:, :extent], out[:, extent:]


def pipeline_kernel(
    depth_count, weight_ref, window_ref, probe_ref, measured_ref, op_ref, grad_ref,
    seen, wave_grad, send_out, recv_out, send_back, recv_back,
):
    slots, _, layers = window_ref.shape[:3]
    depth_at = lax.axis_index("depth")
    last = depth_at // (depth_count - 1)
    first = depth_at == 0
    not_last = depth_at < depth_count - 1
    own_layers = layers - last

    barrier = pltpu.get_barrier_semaphore()

    @pl.when(not_last)
    def _():
        pl.semaphore_signal(barrier, inc=1, device_id={"depth": depth_at + 1}, device_id_type=MESH)

    @pl.when(depth_at > 0)
    def _():
        pl.semaphore_signal(barrier, inc=1, device_id={"depth": depth_at - 1}, device_id_type=MESH)

    pl.semaphore_wait(barrier, 2 - last - (depth_count - 1 - depth_at) // (depth_count - 1))

    def wave_copy(slot):
        return pltpu.make_async_remote_copy(
            src_ref=seen.at[slot, layers], dst_ref=seen.at[slot, 0],
            send_sem=send_out.at[slot], recv_sem=recv_out.at[slot],
            device_id={"depth": depth_at + 1}, device_id_type=MESH,
        )

    def grad_copy(slot):
        return pltpu.make_async_remote_copy(
            src_ref=wave_grad.at[slot, 0], dst_ref=wave_grad.at[slot, layers],
            send_sem=send_back.at[slot], recv_sem=recv_back.at[slot],
            device_id={"depth": depth_at - 1}, device_id_type=MESH,
        )

    def illuminated(slot, layer):
        o_real, o_imag = window_ref[slot, 0, layer], window_ref[slot, 1, layer]
        w_real, w_imag = seen[slot, layer, 0], seen[slot, layer, 1]
        return o_real * w_real - o_imag * w_imag, o_real * w_imag + o_imag * w_real

    def keep_gradients(slot, layer, g_real, g_imag):
        o_real, o_imag = window_ref[slot, 0, layer], window_ref[slot, 1, layer]
        w_real, w_imag = seen[slot, layer, 0], seen[slot, layer, 1]
        wave_grad[slot, layer, 0] = g_real * o_real + g_imag * o_imag
        wave_grad[slot, layer, 1] = g_imag * o_real - g_real * o_imag
        grad_ref[slot, 0, layer] = g_real * w_real + g_imag * w_imag
        grad_ref[slot, 1, layer] = g_imag * w_real - g_real * w_imag

    def go_out(slot):
        @pl.when(first)
        def _():
            seen[slot, 0] = probe_ref[...]

        @pl.when(depth_at > 0)
        def _():
            wave_copy(slot).wait_recv()

        @pl.loop(0, own_layers)
        def _(layer):
            real, imag = transform(*illuminated(slot, layer), op_ref, 0)
            seen[slot, layer + 1, 0] = real
            seen[slot, layer + 1, 1] = imag

        @pl.when(not_last)
        def _():
            wave_copy(slot).start()

        @pl.when(last == 1)
        def _():
            real, imag = transform(*illuminated(slot, layers - 1), op_ref, 2)
            resid = real * real + imag * imag - measured_ref[slot]
            factor = (4.0 * weight_ref[slot]) * resid
            g_real, g_imag = transform(factor * real, factor * imag, op_ref, 3)
            keep_gradients(slot, layers - 1, g_real, g_imag)

    def go_back(slot):
        @pl.when(not_last)
        def _():
            grad_copy(slot).wait_recv()

        @pl.loop(0, own_layers)
        def _(step):
            layer = own_layers - 1 - step
            g_real, g_imag = transform(
                wave_grad[slot, layer + 1, 0], wave_grad[slot, layer + 1, 1], op_ref, 1
            )
            keep_gradients(slot, layer, g_real, g_imag)

        @pl.when(depth_at > 0)
        def _():
            grad_copy(slot).start()

    @pl.loop(0, 2 * slots)
    def _(step):
        backward = last * (step % 2) + (1 - last) * (step // slots)
        slot = last * (step // 2) + (1 - last) * (step % slots)

        @pl.when(backward == 0)
        def _():
            go_out(slot)

        @pl.when(backward == 1)
        def _():
            go_back(slot)

    @pl.loop(0, slots)
    def _(slot):
        @pl.when(not_last)
        def _():
            wave_copy(slot).wait_send()

        @pl.when(depth_at > 0)
        def _():
            grad_copy(slot).wait_send()


def run_pipeline(depth_count, weights, windows, probe, measured, ops):
    slots, _, layers, extent, _ = windows.shape
    whole = pl.BlockSpec(memory_space=pltpu.VMEM)
    return pl.pallas_call(
        functools.partial(pipeline_kernel, depth_count),
        out_shape=jax.ShapeDtypeStruct(windows.shape, jnp.float32),
        in_specs=[pl.BlockSpec(memory_space=pltpu.SMEM), whole, whole, whole, whole],
        out_specs=whole,
        scratch_shapes=[
            pltpu.VMEM((slots, layers + 1, 2, extent, extent), jnp.float32),
            pltpu.VMEM((slots, layers + 1, 2, extent, extent), jnp.float32),
        ]
        + [pltpu.SemaphoreType.DMA((slots,))] * 4,
        compiler_params=pltpu.CompilerParams(
            collective_id=0, has_side_effects=True, vmem_limit_bytes=VMEM_LIMIT
        ),
        name="depth_pipeline",
    )(weights, windows, probe, measured, ops)


def cut_kernel(start_ref, above_ref, strip_ref, below_ref, out_ref):
    extent = out_ref.shape[-1]
    strip = strip_ref[0, 0]
    for slot, parts in enumerate(((above_ref[0, 0], strip), (strip, below_ref[0, 0]))):
        area = jnp.concatenate(parts, 0)
        rows, cols = area.shape
        area = pltpu.roll(area, lax.rem(rows - start_ref[slot, 0], rows), 0)[:extent]
        area = pltpu.roll(area, lax.rem(cols - start_ref[slot, 1], cols), 1)
        out_ref[slot, 0, 0] = area[:, :extent]


def cut_windows(starts, above, strip, below, extent):
    slots = starts.shape[0]
    _, layers, rows, cols = strip.shape
    half = above.shape[2]

    def spec(height):
        return pl.BlockSpec((1, 1, height, cols), lambda c, l: (c, l, 0, 0))

    return pl.pallas_call(
        cut_kernel,
        grid=(2, layers),
        out_shape=jax.ShapeDtypeStruct((slots, 2, layers, extent, extent), jnp.float32),
        in_specs=[pl.BlockSpec(memory_space=pltpu.SMEM), spec(half), spec(rows), spec(half)],
        out_specs=pl.BlockSpec((slots, 1, 1, extent, extent), lambda c, l: (0, c, l, 0, 0)),
        compiler_params=pltpu.CompilerParams(vmem_limit_bytes=VMEM_LIMIT),
        name="cut_windows",
    )(starts, above, strip, below)


def place_kernel(start_ref, grad_ref, above_ref, inner_ref, below_ref):
    half = above_ref.shape[2]
    rows, cols = inner_ref.shape[2:]
    areas = []
    for slot in range(2):
        patch = grad_ref[slot, 0, 0]
        extent = patch.shape[0]
        patch = jnp.concatenate([patch, jnp.zeros((extent, cols - extent), jnp.float32)], 1)
        patch = pltpu.roll(patch, start_ref[slot, 1], 1)
        area = jnp.concatenate([patch, jnp.zeros((rows + half - extent, cols), jnp.float32)], 0)
        areas.append(pltpu.roll(area, start_ref[slot, 0], 0))
    above_ref[0, 0] = areas[0][:half]
    inner_ref[0, 0] = areas[0][half:] + areas[1][:rows]
    below_ref[0, 0] = areas[1][rows:]


def place_gradients(starts, grads, half, rows, cols):
    slots, _, layers, extent, _ = grads.shape

    def spec(height):
        return pl.BlockSpec((1, 1, height, cols), lambda c, l: (c, l, 0, 0))

    def shape(height):
        return jax.ShapeDtypeStruct((2, layers, height, cols), jnp.float32)

    return pl.pallas_call(
        place_kernel,
        grid=(2, layers),
        out_shape=(shape(half), shape(rows), shape(half)),
        in_specs=[
            pl.BlockSpec(memory_space=pltpu.SMEM),
            pl.BlockSpec((slots, 1, 1, extent, extent), lambda c, l: (0, c, l, 0, 0)),
        ],
        out_specs=(spec(half), spec(rows), spec(half)),
        compiler_params=pltpu.CompilerParams(vmem_limit_bytes=VMEM_LIMIT),
        name="place_gradients",
    )(starts, grads)


def shards(transmission, probe, intensity, positions, batch):
    extent = probe.shape[1]
    half = extent // 2
    rows, cols = transmission.shape[2:]
    depth_count = lax.axis_size("depth")
    tiles = lax.axis_size("tile")
    tile_at = lax.axis_index("tile")
    ops = jnp.asarray(operators(extent))
    top_rows = positions[:, 0] - tile_at * rows + half
    starts = jnp.stack([top_rows - jnp.array([0, half], jnp.int32), positions[:, 1]], 1)
    down = [(i, i + 1) for i in range(tiles - 1)]
    up = [(i + 1, i) for i in range(tiles - 1)]

    strip = transmission
    for turn in range(2):
        weights = (batch == turn).astype(jnp.float32)
        above = lax.ppermute(strip[:, :, rows - half :], "tile", down)
        below = lax.ppermute(strip[:, :, :half], "tile", up)
        windows = cut_windows(starts, above, strip, below, extent)
        grads = run_pipeline(depth_count, weights, windows, probe, intensity, ops)
        to_above, inner, to_below = place_gradients(starts, grads, half, rows, cols)
        from_above = lax.ppermute(to_below, "tile", down)
        from_below = lax.ppermute(to_above, "tile", up)
        full = inner + jnp.concatenate([from_above, from_below], 2)
        strip = strip - step_rate * full
    return strip


def solution(mesh):
    return jax.shard_map(
        shards,
        mesh=mesh,
        in_specs=(
            P(None, "depth", "tile", None),
            P(),
            P("tile", None, None),
            P("tile", None),
            P("tile"),
        ),
        out_specs=P(None, "depth", "tile", None),
        check_vma=False,
    )
```

```python
import functools
import math

import jax
import jax.numpy as jnp
import ml_dtypes
import numpy as np
from jax import lax
from jax.experimental import pallas as pl
from jax.experimental.pallas import tpu as pltpu
from jax.sharding import PartitionSpec as P

prop_strength = 24.0
step_rate = 0.08
MESH = pl.DeviceIdType.MESH
VMEM_LIMIT = 48 * 1024 * 1024


def operators(extent):
    counter = np.arange(extent)
    phase = (counter[:, None] * counter[None, :]) % extent
    angles = phase * (2.0 * math.pi / extent)
    fourier = (np.cos(angles) - 1j * np.sin(angles)) / math.sqrt(extent)
    freq = np.where(counter < extent // 2, counter, counter - extent) / extent
    chirp = np.exp(-1j * math.pi * prop_strength * freq * freq)
    forward = np.conj(fourier) @ (chirp[:, None] * fourier)
    forward = 0.5 * (forward + forward.T)
    packed = []
    for matrix in (forward, np.conj(forward), fourier, np.conj(fourier)):
        whole = np.block([[matrix.real, matrix.imag], [-matrix.imag, matrix.real]]).astype(np.float32)
        high = whole.astype(ml_dtypes.bfloat16)
        low = (whole - high.astype(np.float32)).astype(ml_dtypes.bfloat16)
        packed.append(np.stack([high, low]))
    return np.stack(packed)


def split(value):
    high = value.astype(jnp.bfloat16)
    return high, (value - high.astype(jnp.float32)).astype(jnp.bfloat16)


def dot(first, second):
    return jnp.dot(first, second, preferred_element_type=jnp.float32)


def transform(real, imag, op_ref, which):
    extent = real.shape[0]
    real_parts, imag_parts = split(real), split(imag)
    high, low = [
        jnp.concatenate([jnp.concatenate([r, i], 1), jnp.concatenate([-i, r], 1)], 0)
        for r, i in zip(real_parts, imag_parts)
    ]
    left_high, left_low = op_ref[which, 0, :extent], op_ref[which, 1, :extent]
    turned = dot(left_high, high) + (dot(left_high, low) + dot(left_low, high))
    high, low = split(turned)
    right_high, right_low = op_ref[which, 0], op_ref[which, 1]
    out = dot(high, right_high) + (dot(high, right_low) + dot(low, right_high))
    return out[:, :extent], out[:, extent:]


def whole_kernel(
    depth_count, tiles, start_ref, near_ref, weight_ref, object_ref, probe_ref, measured_ref, op_ref, strip_ref,
    window, patch_grad, seen, wave_grad, halo_out, halo_in, rim_out, rim_in,
    wave_send, wave_recv, back_send, back_recv, halo_send, halo_recv, rim_send, rim_recv,
):
    phases, slots, _, _, extent, _ = seen.shape
    layers, rows, cols = object_ref.shape[1:]
    half = extent // 2
    area_rows = half + rows
    depth_at = lax.axis_index("depth")
    tile_at = lax.axis_index("tile")
    last = depth_at // (depth_count - 1)
    not_last = depth_at < depth_count - 1
    has_above = tile_at > 0
    has_below = tile_at < tiles - 1
    own_layers = layers - last
    links = (
        (not_last, {"depth": depth_at + 1}),
        (depth_at > 0, {"depth": depth_at - 1}),
        (has_below, {"tile": tile_at + 1}),
        (has_above, {"tile": tile_at - 1}),
    )
    ends = last + (depth_count - 1 - depth_at) // (depth_count - 1)
    ends = ends + tile_at // (tiles - 1) + (tiles - 1 - tile_at) // (tiles - 1)

    barrier = pltpu.get_barrier_semaphore()
    for there, device in links:

        @pl.when(there)
        def _():
            pl.semaphore_signal(barrier, inc=1, device_id=device, device_id_type=MESH)

    strip_ref[...] = object_ref[...]
    reaches = (has_above, has_below)
    serves = (has_below, has_above)
    for slot in range(2):

        @pl.when(jnp.logical_not(reaches[slot]))
        def _():
            for phase in range(phases):
                halo_in[phase, slot] = jnp.zeros(halo_in.shape[2:], jnp.float32)

        @pl.when(jnp.logical_not(serves[slot]))
        def _():
            for phase in range(phases):
                rim_in[phase, slot] = jnp.zeros(rim_in.shape[2:], jnp.float32)

    pl.semaphore_wait(barrier, 4 - ends)

    def wave_copy(phase, slot):
        return pltpu.make_async_remote_copy(
            src_ref=seen.at[phase, slot, layers], dst_ref=seen.at[phase, slot, 0],
            send_sem=wave_send.at[phase, slot], recv_sem=wave_recv.at[phase, slot],
            device_id=links[0][1], device_id_type=MESH,
        )

    def back_copy(phase, slot):
        return pltpu.make_async_remote_copy(
            src_ref=wave_grad.at[phase, slot, 0], dst_ref=wave_grad.at[phase, slot, layers],
            send_sem=back_send.at[phase, slot], recv_sem=back_recv.at[phase, slot],
            device_id=links[1][1], device_id_type=MESH,
        )

    def halo_copy(phase, side, layer):
        return pltpu.make_async_remote_copy(
            src_ref=halo_out.at[phase, side, layer], dst_ref=halo_in.at[phase, side, layer],
            send_sem=halo_send.at[phase, side, layer], recv_sem=halo_recv.at[phase, side, layer],
            device_id=links[2 + side][1], device_id_type=MESH,
        )

    def rim_copy(phase, slot, layer):
        return pltpu.make_async_remote_copy(
            src_ref=rim_out.at[phase, slot, layer], dst_ref=rim_in.at[phase, slot, layer],
            send_sem=rim_send.at[phase, slot, layer], recv_sem=rim_recv.at[phase, slot, layer],
            device_id=links[3 - slot][1], device_id_type=MESH,
        )

    def send_halo(phase, side, layer):
        base = rows - half if side == 0 else 0
        for part in range(2):
            piece = strip_ref[part, layer, base : base + half]
            piece = pltpu.roll(piece, lax.rem(cols - near_ref[side], cols), 1)
            halo_out[phase, side, layer, part] = piece[:, :extent]

        @pl.when(serves[side])
        def _():
            halo_copy(phase, side, layer).start()

    def cut_window(phase, slot, layer):
        shift = lax.rem(2 * area_rows - start_ref[slot, 0], area_rows)
        for part in range(2):
            own = pltpu.roll(strip_ref[part, layer], lax.rem(cols - start_ref[slot, 1], cols), 1)
            area = jnp.concatenate([halo_in[phase, slot, layer, part], own[:, :extent]], 0)
            window[slot, part, layer] = pltpu.roll(area, shift, 0)[:extent]

    def apply_gradients(phase, slot):
        @pl.loop(0, layers)
        def _(layer):
            for part in range(2):
                patch = patch_grad[slot, part, layer] * step_rate
                area = jnp.concatenate([patch, jnp.zeros((area_rows - extent, extent), jnp.float32)], 0)
                area = pltpu.roll(area, lax.rem(start_ref[slot, 0], area_rows), 0)
                rim_out[phase, slot, layer, part] = area[:half]
                own = jnp.concatenate([area[half:], jnp.zeros((rows, cols - extent), jnp.float32)], 1)
                strip_ref[part, layer] -= pltpu.roll(own, start_ref[slot, 1], 1)

            @pl.when(reaches[slot])
            def _():
                rim_copy(phase, slot, layer).start()

    def take_rim(phase, side, layer):
        @pl.when(serves[side])
        def _():
            rim_copy(phase, side, layer).wait_recv()

        base = rows - half if side == 0 else 0
        for part in range(2):
            piece = rim_in[phase, side, layer, part]
            piece = jnp.concatenate([piece, jnp.zeros((half, cols - extent), jnp.float32)], 1)
            strip_ref[part, layer, base : base + half] -= pltpu.roll(piece, near_ref[side], 1)

    def illuminated(phase, slot, layer):
        o_real, o_imag = window[slot, 0, layer], window[slot, 1, layer]
        w_real, w_imag = seen[phase, slot, layer, 0], seen[phase, slot, layer, 1]
        return o_real * w_real - o_imag * w_imag, o_real * w_imag + o_imag * w_real

    def keep_gradients(phase, slot, layer, g_real, g_imag):
        o_real, o_imag = window[slot, 0, layer], window[slot, 1, layer]
        w_real, w_imag = seen[phase, slot, layer, 0], seen[phase, slot, layer, 1]
        wave_grad[phase, slot, layer, 0] = g_real * o_real + g_imag * o_imag
        wave_grad[phase, slot, layer, 1] = g_imag * o_real - g_real * o_imag
        patch_grad[slot, 0, layer] = g_real * w_real + g_imag * w_imag
        patch_grad[slot, 1, layer] = g_imag * w_real - g_real * w_imag

    def go_out(phase, slot):
        @pl.when(depth_at == 0)
        def _():
            seen[phase, slot, 0] = probe_ref[...]

        @pl.when(depth_at > 0)
        def _():
            wave_copy(phase, slot).wait_recv()

        @pl.loop(0, own_layers)
        def _(layer):
            real, imag = transform(*illuminated(phase, slot, layer), op_ref, 0)
            seen[phase, slot, layer + 1, 0] = real
            seen[phase, slot, layer + 1, 1] = imag

        @pl.when(not_last)
        def _():
            wave_copy(phase, slot).start()

        @pl.when(last == 1)
        def _():
            real, imag = transform(*illuminated(phase, slot, layers - 1), op_ref, 2)
            resid = real * real + imag * imag - measured_ref[slot]
            factor = (4.0 * weight_ref[phase, slot]) * resid
            g_real, g_imag = transform(factor * real, factor * imag, op_ref, 3)
            keep_gradients(phase, slot, layers - 1, g_real, g_imag)

    def go_back(phase, slot):
        @pl.when(not_last)
        def _():
            back_copy(phase, slot).wait_recv()

        @pl.loop(0, own_layers)
        def _(step):
            layer = own_layers - 1 - step
            g_real, g_imag = transform(
                wave_grad[phase, slot, layer + 1, 0], wave_grad[phase, slot, layer + 1, 1], op_ref, 1
            )
            keep_gradients(phase, slot, layer, g_real, g_imag)

        @pl.when(depth_at > 0)
        def _():
            back_copy(phase, slot).start()

    @pl.loop(0, layers)
    def _(layer):
        for side in range(2):
            send_halo(0, side, layer)

    @pl.loop(0, phases)
    def _(phase):
        @pl.loop(0, layers)
        def _(layer):
            for slot in range(2):

                @pl.when(reaches[slot])
                def _():
                    halo_copy(phase, slot, layer).wait_recv()

                cut_window(phase, slot, layer)

        @pl.loop(0, 2 * slots)
        def _(step):
            backward = last * (step % 2) + (1 - last) * (step // slots)
            slot_at = last * (step // 2) + (1 - last) * (step % slots)

            @pl.when(backward == 0)
            def _():
                go_out(phase, slot_at)

            @pl.when(backward == 1)
            def _():
                go_back(phase, slot_at)
                for slot in range(2):

                    @pl.when(slot_at == slot)
                    def _():
                        apply_gradients(phase, slot)

        @pl.loop(0, layers)
        def _(layer):
            for side in range(2):
                take_rim(phase, side, layer)

                @pl.when(phase < phases - 1)
                def _():
                    send_halo(phase + 1, side, layer)

    @pl.loop(0, phases)
    def _(phase):
        for slot in range(2):

            @pl.when(not_last)
            def _():
                wave_copy(phase, slot).wait_send()

            @pl.when(depth_at > 0)
            def _():
                back_copy(phase, slot).wait_send()

            @pl.loop(0, layers)
            def _(layer):
                @pl.when(serves[slot])
                def _():
                    halo_copy(phase, slot, layer).wait_send()

                @pl.when(reaches[slot])
                def _():
                    rim_copy(phase, slot, layer).wait_send()


def shards(transmission, probe, intensity, positions, batch):
    extent = probe.shape[1]
    half = extent // 2
    slots = intensity.shape[0]
    _, layers, rows, _ = transmission.shape
    depth_count = lax.axis_size("depth")
    tiles = lax.axis_size("tile")
    tile_at = lax.axis_index("tile")
    phases = 2
    ops = jnp.asarray(operators(extent))
    top_rows = positions[:, 0] - tile_at * rows + half
    starts = jnp.stack([top_rows, positions[:, 1]], 1)
    near = jnp.concatenate([
        lax.ppermute(positions[:1, 1], "tile", [(i + 1, i) for i in range(tiles - 1)]),
        lax.ppermute(positions[1:, 1], "tile", [(i, i + 1) for i in range(tiles - 1)]),
    ])
    weights = (batch[None] == jnp.arange(phases, dtype=batch.dtype)[:, None]).astype(jnp.float32)
    whole = pl.BlockSpec(memory_space=pltpu.VMEM)
    scalars = pl.BlockSpec(memory_space=pltpu.SMEM)
    edge = pltpu.VMEM((phases, 2, layers, 2, half, extent), jnp.float32)
    waves = pltpu.VMEM((phases, slots, layers + 1, 2, extent, extent), jnp.float32)
    patches = pltpu.VMEM((slots, 2, layers, extent, extent), jnp.float32)
    return pl.pallas_call(
        functools.partial(whole_kernel, depth_count, tiles),
        out_shape=jax.ShapeDtypeStruct(transmission.shape, jnp.float32),
        in_specs=[scalars, scalars, scalars, whole, whole, whole, whole],
        out_specs=whole,
        scratch_shapes=[patches, patches, waves, waves, edge, edge, edge, edge]
        + [pltpu.SemaphoreType.DMA((phases, slots))] * 4
        + [pltpu.SemaphoreType.DMA((phases, slots, layers))] * 4,
        compiler_params=pltpu.CompilerParams(
            collective_id=0, has_side_effects=True, vmem_limit_bytes=VMEM_LIMIT
        ),
        name="two_minibatches",
    )(starts, near, weights, transmission, probe, intensity, ops)


def solution(mesh):
    return jax.shard_map(
        shards,
        mesh=mesh,
        in_specs=(
            P(None, "depth", "tile", None),
            P(),
            P("tile", None, None),
            P("tile", None),
            P("tile"),
        ),
        out_specs=P(None, "depth", "tile", None),
        check_vma=False,
    )
```

```python
import functools
import math

import jax
import jax.numpy as jnp
import ml_dtypes
import numpy as np
from jax import lax
from jax.experimental import pallas as pl
from jax.experimental.pallas import tpu as pltpu
from jax.sharding import PartitionSpec as P

prop_strength = 24.0
step_rate = 0.08
MESH = pl.DeviceIdType.MESH
VMEM_LIMIT = 48 * 1024 * 1024


def operators(extent):
    counter = np.arange(extent)
    phase = (counter[:, None] * counter[None, :]) % extent
    angles = phase * (2.0 * math.pi / extent)
    fourier = (np.cos(angles) - 1j * np.sin(angles)) / math.sqrt(extent)
    freq = np.where(counter < extent // 2, counter, counter - extent) / extent
    chirp = np.exp(-1j * math.pi * prop_strength * freq * freq)
    forward = np.conj(fourier) @ (chirp[:, None] * fourier)
    forward = 0.5 * (forward + forward.T)
    packed = []
    for matrix in (forward, np.conj(forward), fourier, np.conj(fourier)):
        whole = np.block([[matrix.real, matrix.imag], [-matrix.imag, matrix.real]]).astype(np.float32)
        high = whole.astype(ml_dtypes.bfloat16)
        low = (whole - high.astype(np.float32)).astype(ml_dtypes.bfloat16)
        packed.append(np.stack([high, low]))
    return np.stack(packed)


def split(value):
    high = value.astype(jnp.bfloat16)
    return high, (value - high.astype(jnp.float32)).astype(jnp.bfloat16)


def dot(first, second):
    return jnp.dot(first, second, preferred_element_type=jnp.float32)


def transform(real, imag, op_ref, which):
    extent = real.shape[0]
    real_parts, imag_parts = split(real), split(imag)
    high, low = [
        jnp.concatenate([jnp.concatenate([r, i], 1), jnp.concatenate([-i, r], 1)], 0)
        for r, i in zip(real_parts, imag_parts)
    ]
    left_high, left_low = op_ref[which, 0, :extent], op_ref[which, 1, :extent]
    turned = dot(left_high, high) + (dot(left_high, low) + dot(left_low, high))
    high, low = split(turned)
    right_high, right_low = op_ref[which, 0], op_ref[which, 1]
    out = dot(high, right_high) + (dot(high, right_low) + dot(low, right_high))
    return out[:, :extent], out[:, extent:]


def whole_kernel(
    depth_count, tiles, start_ref, near_ref, weight_ref, object_ref, probe_ref, measured_ref, op_ref, strip_ref,
    window, patch_grad, seen, wave_grad, halo_out, halo_in, rim_out, rim_in,
    wave_send, wave_recv, back_send, back_recv, halo_send, halo_recv, rim_send, rim_recv, turn,
):
    phases, slots, _, _, extent, _ = seen.shape
    layers, rows, cols = object_ref.shape[1:]
    half = extent // 2
    area_rows = half + rows
    depth_at = lax.axis_index("depth")
    tile_at = lax.axis_index("tile")
    last = depth_at // (depth_count - 1)
    not_last = depth_at < depth_count - 1
    has_above = tile_at > 0
    has_below = tile_at < tiles - 1
    own_layers = layers - last
    parity = tile_at % 2
    partner = tile_at + 1 - 2 * parity
    links = (
        (not_last, {"depth": depth_at + 1}),
        (depth_at > 0, {"depth": depth_at - 1}),
        (has_below, {"tile": tile_at + 1}),
        (has_above, {"tile": tile_at - 1}),
    )
    start_depth = (depth_count - 1 - depth_at) // (depth_count - 1)
    ends = last + start_depth
    ends = ends + tile_at // (tiles - 1) + (tiles - 1 - tile_at) // (tiles - 1)

    barrier = pltpu.get_barrier_semaphore()
    for there, device in links:

        @pl.when(there)
        def _():
            pl.semaphore_signal(barrier, inc=1, device_id=device, device_id_type=MESH)

    strip_ref[...] = object_ref[...]
    reaches = (has_above, has_below)
    serves = (has_below, has_above)
    for slot in range(2):

        @pl.when(jnp.logical_not(reaches[slot]))
        def _():
            for phase in range(phases):
                halo_in[phase, slot] = jnp.zeros(halo_in.shape[2:], jnp.float32)

        @pl.when(jnp.logical_not(serves[slot]))
        def _():
            for phase in range(phases):
                rim_in[phase, slot] = jnp.zeros(rim_in.shape[2:], jnp.float32)

    pl.semaphore_wait(barrier, 4 - ends)

    def wave_copy(phase, slot):
        return pltpu.make_async_remote_copy(
            src_ref=seen.at[phase, slot, layers], dst_ref=seen.at[phase, slot, 0],
            send_sem=wave_send.at[phase, slot], recv_sem=wave_recv.at[phase, slot],
            device_id=links[0][1], device_id_type=MESH,
        )

    def back_copy(phase, slot):
        return pltpu.make_async_remote_copy(
            src_ref=wave_grad.at[phase, slot, 0], dst_ref=wave_grad.at[phase, slot, layers],
            send_sem=back_send.at[phase, slot], recv_sem=back_recv.at[phase, slot],
            device_id=links[1][1], device_id_type=MESH,
        )

    def halo_copy(phase, side, layer):
        return pltpu.make_async_remote_copy(
            src_ref=halo_out.at[phase, side, layer], dst_ref=halo_in.at[phase, side, layer],
            send_sem=halo_send.at[phase, side, layer], recv_sem=halo_recv.at[phase, side, layer],
            device_id=links[2 + side][1], device_id_type=MESH,
        )

    def rim_copy(phase, slot, layer):
        return pltpu.make_async_remote_copy(
            src_ref=rim_out.at[phase, slot, layer], dst_ref=rim_in.at[phase, slot, layer],
            send_sem=rim_send.at[phase, slot, layer], recv_sem=rim_recv.at[phase, slot, layer],
            device_id=links[3 - slot][1], device_id_type=MESH,
        )

    def send_halo(phase, side, layer):
        base = rows - half if side == 0 else 0
        for part in range(2):
            piece = strip_ref[part, layer, base : base + half]
            piece = pltpu.roll(piece, lax.rem(cols - near_ref[side], cols), 1)
            halo_out[phase, side, layer, part] = piece[:, :extent]

        @pl.when(serves[side])
        def _():
            halo_copy(phase, side, layer).start()

    def cut_window(phase, slot, layer):
        shift = lax.rem(2 * area_rows - start_ref[slot, 0], area_rows)
        for part in range(2):
            own = pltpu.roll(strip_ref[part, layer], lax.rem(cols - start_ref[slot, 1], cols), 1)
            area = jnp.concatenate([halo_in[phase, slot, layer, part], own[:, :extent]], 0)
            window[slot, part, layer] = pltpu.roll(area, shift, 0)[:extent]

    def apply_gradients(phase, slot):
        @pl.loop(0, layers)
        def _(layer):
            for part in range(2):
                patch = patch_grad[slot, part, layer] * step_rate
                area = jnp.concatenate([patch, jnp.zeros((area_rows - extent, extent), jnp.float32)], 0)
                area = pltpu.roll(area, lax.rem(start_ref[slot, 0], area_rows), 0)
                rim_out[phase, slot, layer, part] = area[:half]
                own = jnp.concatenate([area[half:], jnp.zeros((rows, cols - extent), jnp.float32)], 1)
                strip_ref[part, layer] -= pltpu.roll(own, start_ref[slot, 1], 1)

            @pl.when(reaches[slot])
            def _():
                rim_copy(phase, slot, layer).start()

    def take_rim(phase, side, layer):
        @pl.when(serves[side])
        def _():
            rim_copy(phase, side, layer).wait_recv()

        base = rows - half if side == 0 else 0
        for part in range(2):
            piece = rim_in[phase, side, layer, part]
            piece = jnp.concatenate([piece, jnp.zeros((half, cols - extent), jnp.float32)], 1)
            strip_ref[part, layer, base : base + half] -= pltpu.roll(piece, near_ref[side], 1)

    def illuminated(phase, slot, layer):
        o_real, o_imag = window[slot, 0, layer], window[slot, 1, layer]
        w_real, w_imag = seen[phase, slot, layer, 0], seen[phase, slot, layer, 1]
        return o_real * w_real - o_imag * w_imag, o_real * w_imag + o_imag * w_real

    def keep_gradients(phase, slot, layer, g_real, g_imag):
        o_real, o_imag = window[slot, 0, layer], window[slot, 1, layer]
        w_real, w_imag = seen[phase, slot, layer, 0], seen[phase, slot, layer, 1]
        wave_grad[phase, slot, layer, 0] = g_real * o_real + g_imag * o_imag
        wave_grad[phase, slot, layer, 1] = g_imag * o_real - g_real * o_imag
        patch_grad[slot, 0, layer] = g_real * w_real + g_imag * w_imag
        patch_grad[slot, 1, layer] = g_imag * w_real - g_real * w_imag

    def pass_turn(phase, slot):
        wave_copy(phase, slot).wait_send()

        @pl.when((parity == 0) | (slot < slots - 1))
        def _():
            pl.semaphore_signal(turn, inc=1, device_id={"tile": partner}, device_id_type=MESH)

    def send_in_turn(phase, slot):
        @pl.when(slot > 0)
        def _():
            pass_turn(phase, slot - 1)

        @pl.when((parity == 1) | (slot > 0))
        def _():
            pl.semaphore_wait(turn, 1)

        wave_copy(phase, slot).start()

        @pl.when(slot == slots - 1)
        def _():
            pass_turn(phase, slot)

    def go_out(phase, slot):
        @pl.when(depth_at == 0)
        def _():
            seen[phase, slot, 0] = probe_ref[...]

        @pl.when(depth_at > 0)
        def _():
            wave_copy(phase, slot).wait_recv()

        @pl.loop(0, own_layers)
        def _(layer):
            real, imag = transform(*illuminated(phase, slot, layer), op_ref, 0)
            seen[phase, slot, layer + 1, 0] = real
            seen[phase, slot, layer + 1, 1] = imag

        @pl.when(depth_at == 0)
        def _():
            send_in_turn(phase, slot)

        @pl.when(not_last & (depth_at > 0))
        def _():
            wave_copy(phase, slot).start()

        @pl.when(last == 1)
        def _():
            real, imag = transform(*illuminated(phase, slot, layers - 1), op_ref, 2)
            resid = real * real + imag * imag - measured_ref[slot]
            factor = (4.0 * weight_ref[phase, slot]) * resid
            g_real, g_imag = transform(factor * real, factor * imag, op_ref, 3)
            keep_gradients(phase, slot, layers - 1, g_real, g_imag)

    def go_back(phase, slot):
        @pl.when(not_last)
        def _():
            back_copy(phase, slot).wait_recv()

        @pl.loop(0, own_layers)
        def _(step):
            layer = own_layers - 1 - step
            g_real, g_imag = transform(
                wave_grad[phase, slot, layer + 1, 0], wave_grad[phase, slot, layer + 1, 1], op_ref, 1
            )
            keep_gradients(phase, slot, layer, g_real, g_imag)

        @pl.when(depth_at > 0)
        def _():
            back_copy(phase, slot).start()

    @pl.loop(0, layers)
    def _(layer):
        for side in range(2):
            send_halo(0, side, layer)

    @pl.loop(0, phases)
    def _(phase):
        @pl.loop(0, 2 * slots)
        def _(step):
            backward = last * (step % 2) + (1 - last) * (step // slots)
            slot_at = last * (step // 2) + (1 - last) * (step % slots)

            @pl.when((step < slots) & ((start_depth == 1) | (step == 0)))
            def _():
                @pl.loop(step, step + 1 + (1 - start_depth) * (slots - 1))
                def _(cut_slot):
                    @pl.loop(0, layers)
                    def _(layer):
                        for slot in range(2):

                            @pl.when((cut_slot == slot) & reaches[slot])
                            def _():
                                halo_copy(phase, slot, layer).wait_recv()

                        cut_window(phase, cut_slot, layer)

            @pl.when(backward == 0)
            def _():
                go_out(phase, slot_at)

            @pl.when(backward == 1)
            def _():
                go_back(phase, slot_at)
                for slot in range(2):

                    @pl.when(slot_at == slot)
                    def _():
                        apply_gradients(phase, slot)

        for side in range(2):

            @pl.loop(0, layers)
            def _(layer):
                take_rim(phase, side, layer)

                @pl.when(phase < phases - 1)
                def _():
                    send_halo(phase + 1, side, layer)

    @pl.loop(0, phases)
    def _(phase):
        for slot in range(2):

            @pl.when(not_last & (depth_at > 0))
            def _():
                wave_copy(phase, slot).wait_send()

            @pl.when(depth_at > 0)
            def _():
                back_copy(phase, slot).wait_send()

            @pl.loop(0, layers)
            def _(layer):
                @pl.when(serves[slot])
                def _():
                    halo_copy(phase, slot, layer).wait_send()

                @pl.when(reaches[slot])
                def _():
                    rim_copy(phase, slot, layer).wait_send()


def shards(transmission, probe, intensity, positions, batch):
    extent = probe.shape[1]
    half = extent // 2
    slots = intensity.shape[0]
    _, layers, rows, _ = transmission.shape
    depth_count = lax.axis_size("depth")
    tiles = lax.axis_size("tile")
    tile_at = lax.axis_index("tile")
    phases = 2
    ops = jnp.asarray(operators(extent))
    top_rows = positions[:, 0] - tile_at * rows + half
    starts = jnp.stack([top_rows, positions[:, 1]], 1)
    near = jnp.concatenate([
        lax.ppermute(positions[:1, 1], "tile", [(i + 1, i) for i in range(tiles - 1)]),
        lax.ppermute(positions[1:, 1], "tile", [(i, i + 1) for i in range(tiles - 1)]),
    ])
    weights = (batch[None] == jnp.arange(phases, dtype=batch.dtype)[:, None]).astype(jnp.float32)
    whole = pl.BlockSpec(memory_space=pltpu.VMEM)
    scalars = pl.BlockSpec(memory_space=pltpu.SMEM)
    edge = pltpu.VMEM((phases, 2, layers, 2, half, extent), jnp.float32)
    waves = pltpu.VMEM((phases, slots, layers + 1, 2, extent, extent), jnp.float32)
    patches = pltpu.VMEM((slots, 2, layers, extent, extent), jnp.float32)
    return pl.pallas_call(
        functools.partial(whole_kernel, depth_count, tiles),
        out_shape=jax.ShapeDtypeStruct(transmission.shape, jnp.float32),
        in_specs=[scalars, scalars, scalars, whole, whole, whole, whole],
        out_specs=whole,
        scratch_shapes=[patches, patches, waves, waves, edge, edge, edge, edge]
        + [pltpu.SemaphoreType.DMA((phases, slots))] * 4
        + [pltpu.SemaphoreType.DMA((phases, slots, layers))] * 4
        + [pltpu.SemaphoreType.REGULAR],
        compiler_params=pltpu.CompilerParams(
            collective_id=0, has_side_effects=True, vmem_limit_bytes=VMEM_LIMIT
        ),
        name="two_minibatches",
    )(starts, near, weights, transmission, probe, intensity, ops)


def solution(mesh):
    return jax.shard_map(
        shards,
        mesh=mesh,
        in_specs=(
            P(None, "depth", "tile", None),
            P(),
            P("tile", None, None),
            P("tile", None),
            P("tile"),
        ),
        out_specs=P(None, "depth", "tile", None),
        check_vma=False,
    )
```

```python
import functools
import math

import jax
import jax.numpy as jnp
import ml_dtypes
import numpy as np
from jax import lax
from jax.experimental import pallas as pl
from jax.experimental.pallas import tpu as pltpu
from jax.sharding import PartitionSpec as P

prop_strength = 24.0
step_rate = 0.08
MESH = pl.DeviceIdType.MESH
CHUNK = 128
VMEM_LIMIT = 48 * 1024 * 1024


def operators(extent):
    order = np.arange(2 * extent).reshape(2, extent // CHUNK, CHUNK).swapaxes(0, 1).reshape(-1)
    counter = np.arange(extent)
    phase = (counter[:, None] * counter[None, :]) % extent
    angles = phase * (2.0 * math.pi / extent)
    fourier = (np.cos(angles) - 1j * np.sin(angles)) / math.sqrt(extent)
    freq = np.where(counter < extent // 2, counter, counter - extent) / extent
    chirp = np.exp(-1j * math.pi * prop_strength * freq * freq)
    forward = np.conj(fourier) @ (chirp[:, None] * fourier)
    forward = 0.5 * (forward + forward.T)
    packed = []
    for matrix in (forward, np.conj(forward), fourier, np.conj(fourier)):
        whole = np.block([[matrix.real, matrix.imag], [-matrix.imag, matrix.real]]).astype(np.float32)
        whole = whole[order][:, order]
        high = whole.astype(ml_dtypes.bfloat16)
        low = (whole - high.astype(np.float32)).astype(ml_dtypes.bfloat16)
        packed.append(np.stack([high, low]))
    return np.stack(packed)


def split(value):
    high = value.astype(jnp.bfloat16)
    return high, (value - high.astype(jnp.float32)).astype(jnp.bfloat16)


def dot(first, second):
    return jnp.dot(first, second, preferred_element_type=jnp.float32)


def left_product(real, imag, op_ref, which):
    extent = real.shape[0]
    pieces = range(0, extent, CHUNK)
    parts = []
    for r, i in zip(split(real), split(imag)):
        upper, lower = jnp.concatenate([r, i], 1), jnp.concatenate([-i, r], 1)
        parts.append(jnp.concatenate([x[at : at + CHUNK] for at in pieces for x in (upper, lower)], 0))
    high, low = [
        jnp.concatenate([op_ref[which, k, 2 * at : 2 * at + CHUNK] for at in pieces], 0) for k in range(2)
    ]
    return dot(jnp.concatenate([high, high, low], 1), jnp.concatenate([parts[0], parts[1], parts[0]], 0))


def transform(get, put, op_ref, which):
    extent = op_ref.shape[-1] // 2
    chunks = range(extent // CHUNK)
    turned = jnp.concatenate([left_product(*get(c), op_ref, which) for c in chunks], 1)
    high, low = split(turned)
    wide = jnp.concatenate([high, high, low], 1)
    for c in chunks:
        columns = slice(2 * c * CHUNK, 2 * (c + 1) * CHUNK)
        right_high, right_low = op_ref[which, 0, :, columns], op_ref[which, 1, :, columns]
        out = dot(wide, jnp.concatenate([right_high, right_low, right_high], 0))
        put(c, out[:, :CHUNK], out[:, CHUNK:])


def strip_of(c):
    return slice(c * CHUNK, (c + 1) * CHUNK)


def whole_kernel(
    depth_count, tiles, start_ref, near_ref, weight_ref, object_ref, probe_ref, measured_ref, op_ref, strip_ref,
    window, patch_grad, seen, wave_grad, halo_out, halo_in, rim_out, rim_in,
    wave_send, wave_recv, back_send, back_recv, halo_send, halo_recv, rim_send, rim_recv,
):
    phases, slots, _, _, extent, _ = seen.shape
    layers, rows, cols = object_ref.shape[1:]
    half = extent // 2
    chunks = extent // CHUNK
    area_rows = half + rows
    depth_at = lax.axis_index("depth")
    tile_at = lax.axis_index("tile")
    last = depth_at // (depth_count - 1)
    not_last = depth_at < depth_count - 1
    has_above = tile_at > 0
    has_below = tile_at < tiles - 1
    own_layers = layers - last
    links = (
        (not_last, {"depth": depth_at + 1}),
        (depth_at > 0, {"depth": depth_at - 1}),
        (has_below, {"tile": tile_at + 1}),
        (has_above, {"tile": tile_at - 1}),
    )
    start_depth = (depth_count - 1 - depth_at) // (depth_count - 1)
    ends = last + start_depth
    ends = ends + tile_at // (tiles - 1) + (tiles - 1 - tile_at) // (tiles - 1)

    barrier = pltpu.get_barrier_semaphore()
    for there, device in links:

        @pl.when(there)
        def _():
            pl.semaphore_signal(barrier, inc=1, device_id=device, device_id_type=MESH)

    strip_ref[...] = object_ref[...]
    reaches = (has_above, has_below)
    serves = (has_below, has_above)
    for slot in range(2):

        @pl.when(jnp.logical_not(reaches[slot]))
        def _():
            for phase in range(phases):
                halo_in[phase, slot] = jnp.zeros(halo_in.shape[2:], jnp.float32)

        @pl.when(jnp.logical_not(serves[slot]))
        def _():
            for phase in range(phases):
                rim_in[phase, slot] = jnp.zeros(rim_in.shape[2:], jnp.float32)

    pl.semaphore_wait(barrier, 4 - ends)

    def wave_copy(phase, slot, c):
        columns = pl.ds(c * CHUNK, CHUNK)
        return pltpu.make_async_remote_copy(
            src_ref=seen.at[phase, slot, layers, :, :, columns], dst_ref=seen.at[phase, slot, 0, :, :, columns],
            send_sem=wave_send.at[phase, slot, c], recv_sem=wave_recv.at[phase, slot, c],
            device_id=links[0][1], device_id_type=MESH,
        )

    def back_copy(phase, slot, c):
        columns = pl.ds(c * CHUNK, CHUNK)
        return pltpu.make_async_remote_copy(
            src_ref=wave_grad.at[phase, slot, 0, :, :, columns],
            dst_ref=wave_grad.at[phase, slot, layers, :, :, columns],
            send_sem=back_send.at[phase, slot, c], recv_sem=back_recv.at[phase, slot, c],
            device_id=links[1][1], device_id_type=MESH,
        )

    def halo_copy(phase, side, layer):
        return pltpu.make_async_remote_copy(
            src_ref=halo_out.at[phase, side, layer], dst_ref=halo_in.at[phase, side, layer],
            send_sem=halo_send.at[phase, side, layer], recv_sem=halo_recv.at[phase, side, layer],
            device_id=links[2 + side][1], device_id_type=MESH,
        )

    def rim_copy(phase, slot, layer):
        return pltpu.make_async_remote_copy(
            src_ref=rim_out.at[phase, slot, layer], dst_ref=rim_in.at[phase, slot, layer],
            send_sem=rim_send.at[phase, slot, layer], recv_sem=rim_recv.at[phase, slot, layer],
            device_id=links[3 - slot][1], device_id_type=MESH,
        )

    def send_halo(phase, side, layer):
        base = rows - half if side == 0 else 0
        for part in range(2):
            piece = strip_ref[part, layer, base : base + half]
            piece = pltpu.roll(piece, lax.rem(cols - near_ref[side], cols), 1)
            halo_out[phase, side, layer, part] = piece[:, :extent]

        @pl.when(serves[side])
        def _():
            halo_copy(phase, side, layer).start()

    def cut_window(phase, slot, layer):
        shift = lax.rem(2 * area_rows - start_ref[slot, 0], area_rows)
        for part in range(2):
            own = pltpu.roll(strip_ref[part, layer], lax.rem(cols - start_ref[slot, 1], cols), 1)
            area = jnp.concatenate([halo_in[phase, slot, layer, part], own[:, :extent]], 0)
            window[slot, part, layer] = pltpu.roll(area, shift, 0)[:extent]

    def apply_gradients(phase, slot):
        @pl.loop(0, layers)
        def _(layer):
            for part in range(2):
                patch = patch_grad[slot, part, layer] * step_rate
                area = jnp.concatenate([patch, jnp.zeros((area_rows - extent, extent), jnp.float32)], 0)
                area = pltpu.roll(area, lax.rem(start_ref[slot, 0], area_rows), 0)
                rim_out[phase, slot, layer, part] = area[:half]
                own = jnp.concatenate([area[half:], jnp.zeros((rows, cols - extent), jnp.float32)], 1)
                strip_ref[part, layer] -= pltpu.roll(own, start_ref[slot, 1], 1)

            @pl.when(reaches[slot])
            def _():
                rim_copy(phase, slot, layer).start()

    def take_rim(phase, side, layer):
        @pl.when(serves[side])
        def _():
            rim_copy(phase, side, layer).wait_recv()

        base = rows - half if side == 0 else 0
        for part in range(2):
            piece = rim_in[phase, side, layer, part]
            piece = jnp.concatenate([piece, jnp.zeros((half, cols - extent), jnp.float32)], 1)
            strip_ref[part, layer, base : base + half] -= pltpu.roll(piece, near_ref[side], 1)

    def illuminated(phase, slot, layer, c):
        at = strip_of(c)
        o_real, o_imag = window[slot, 0, layer, :, at], window[slot, 1, layer, :, at]
        w_real, w_imag = seen[phase, slot, layer, 0, :, at], seen[phase, slot, layer, 1, :, at]
        return o_real * w_real - o_imag * w_imag, o_real * w_imag + o_imag * w_real

    def keep_gradients(phase, slot, layer, c, g_real, g_imag):
        at = strip_of(c)
        o_real, o_imag = window[slot, 0, layer, :, at], window[slot, 1, layer, :, at]
        w_real, w_imag = seen[phase, slot, layer, 0, :, at], seen[phase, slot, layer, 1, :, at]
        wave_grad[phase, slot, layer, 0, :, at] = g_real * o_real + g_imag * o_imag
        wave_grad[phase, slot, layer, 1, :, at] = g_imag * o_real - g_real * o_imag
        patch_grad[slot, 0, layer, :, at] = g_real * w_real + g_imag * w_imag
        patch_grad[slot, 1, layer, :, at] = g_imag * w_real - g_real * w_imag

    def go_out(phase, slot):
        @pl.when(depth_at == 0)
        def _():
            seen[phase, slot, 0] = probe_ref[...]

        @pl.loop(0, own_layers)
        def _(layer):
            def get(c):
                @pl.when((layer == 0) & (depth_at > 0))
                def _():
                    wave_copy(phase, slot, c).wait_recv()

                return illuminated(phase, slot, layer, c)

            def put(c, real, imag):
                seen[phase, slot, layer + 1, 0, :, strip_of(c)] = real
                seen[phase, slot, layer + 1, 1, :, strip_of(c)] = imag

                @pl.when((layer == layers - 1) & not_last)
                def _():
                    wave_copy(phase, slot, c).start()

            transform(get, put, op_ref, 0)

        @pl.when(last == 1)
        def _():
            if layers == 1:
                for c in range(chunks):
                    wave_copy(phase, slot, c).wait_recv()
            far = {}

            def keep(c, real, imag):
                resid = real * real + imag * imag - measured_ref[slot, :, strip_of(c)]
                factor = (4.0 * weight_ref[phase, slot]) * resid
                far[c] = (factor * real, factor * imag)

            transform(functools.partial(illuminated, phase, slot, layers - 1), keep, op_ref, 2)
            transform(far.get, functools.partial(keep_gradients, phase, slot, layers - 1), op_ref, 3)

    def go_back(phase, slot):
        @pl.loop(0, own_layers)
        def _(step):
            layer = own_layers - 1 - step

            def get(c):
                @pl.when((layer == layers - 1) & not_last)
                def _():
                    back_copy(phase, slot, c).wait_recv()

                at = strip_of(c)
                return wave_grad[phase, slot, layer + 1, 0, :, at], wave_grad[phase, slot, layer + 1, 1, :, at]

            def put(c, g_real, g_imag):
                keep_gradients(phase, slot, layer, c, g_real, g_imag)

                @pl.when((layer == 0) & (depth_at > 0))
                def _():
                    back_copy(phase, slot, c).start()

            transform(get, put, op_ref, 1)

    @pl.loop(0, layers)
    def _(layer):
        for side in range(2):
            send_halo(0, side, layer)

    @pl.loop(0, phases)
    def _(phase):
        @pl.loop(0, 2 * slots)
        def _(step):
            backward = last * (step % 2) + (1 - last) * (step // slots)
            slot_at = last * (step // 2) + (1 - last) * (step % slots)

            @pl.when((step < slots) & ((start_depth == 1) | (step == 0)))
            def _():
                @pl.loop(step, step + 1 + (1 - start_depth) * (slots - 1))
                def _(cut_slot):
                    @pl.loop(0, layers)
                    def _(layer):
                        for slot in range(2):

                            @pl.when((cut_slot == slot) & reaches[slot])
                            def _():
                                halo_copy(phase, slot, layer).wait_recv()

                        cut_window(phase, cut_slot, layer)

            @pl.when(backward == 0)
            def _():
                go_out(phase, slot_at)

            @pl.when(backward == 1)
            def _():
                go_back(phase, slot_at)
                for slot in range(2):

                    @pl.when(slot_at == slot)
                    def _():
                        apply_gradients(phase, slot)

        for side in range(2):

            @pl.loop(0, layers)
            def _(layer):
                take_rim(phase, side, layer)

                @pl.when(phase < phases - 1)
                def _():
                    send_halo(phase + 1, side, layer)

    @pl.loop(0, phases)
    def _(phase):
        for slot in range(2):

            for c in range(chunks):

                @pl.when(not_last)
                def _():
                    wave_copy(phase, slot, c).wait_send()

                @pl.when(depth_at > 0)
                def _():
                    back_copy(phase, slot, c).wait_send()

            @pl.loop(0, layers)
            def _(layer):
                @pl.when(serves[slot])
                def _():
                    halo_copy(phase, slot, layer).wait_send()

                @pl.when(reaches[slot])
                def _():
                    rim_copy(phase, slot, layer).wait_send()


def shards(transmission, probe, intensity, positions, batch):
    extent = probe.shape[1]
    half = extent // 2
    slots = intensity.shape[0]
    _, layers, rows, _ = transmission.shape
    depth_count = lax.axis_size("depth")
    tiles = lax.axis_size("tile")
    tile_at = lax.axis_index("tile")
    phases = 2
    ops = jnp.asarray(operators(extent))
    top_rows = positions[:, 0] - tile_at * rows + half
    starts = jnp.stack([top_rows, positions[:, 1]], 1)
    near = jnp.concatenate([
        lax.ppermute(positions[:1, 1], "tile", [(i + 1, i) for i in range(tiles - 1)]),
        lax.ppermute(positions[1:, 1], "tile", [(i, i + 1) for i in range(tiles - 1)]),
    ])
    weights = (batch[None] == jnp.arange(phases, dtype=batch.dtype)[:, None]).astype(jnp.float32)
    whole = pl.BlockSpec(memory_space=pltpu.VMEM)
    scalars = pl.BlockSpec(memory_space=pltpu.SMEM)
    edge = pltpu.VMEM((phases, 2, layers, 2, half, extent), jnp.float32)
    waves = pltpu.VMEM((phases, slots, layers + 1, 2, extent, extent), jnp.float32)
    patches = pltpu.VMEM((slots, 2, layers, extent, extent), jnp.float32)
    return pl.pallas_call(
        functools.partial(whole_kernel, depth_count, tiles),
        out_shape=jax.ShapeDtypeStruct(transmission.shape, jnp.float32),
        in_specs=[scalars, scalars, scalars, whole, whole, whole, whole],
        out_specs=whole,
        scratch_shapes=[patches, patches, waves, waves, edge, edge, edge, edge]
        + [pltpu.SemaphoreType.DMA((phases, slots, extent // CHUNK))] * 4
        + [pltpu.SemaphoreType.DMA((phases, slots, layers))] * 4,
        compiler_params=pltpu.CompilerParams(
            collective_id=0, has_side_effects=True, vmem_limit_bytes=VMEM_LIMIT
        ),
        name="two_minibatches",
    )(starts, near, weights, transmission, probe, intensity, ops)


def solution(mesh):
    return jax.shard_map(
        shards,
        mesh=mesh,
        in_specs=(
            P(None, "depth", "tile", None),
            P(),
            P("tile", None, None),
            P("tile", None),
            P("tile"),
        ),
        out_specs=P(None, "depth", "tile", None),
        check_vma=False,
    )
```
